512 devices in a mesh: row: 32 (over x, y, core), col: 16 (over z).
Axes of the slice: x: 4, y: 4, z: 16, core: 2. Of those that a mesh axis runs over, the one named last changes fastest.
Arguments:
- tokens: bfloat16 [512, 12288], P('col', 'row'), may hold values from -6 to 6
- cotangent: bfloat16 [512, 12288], P('col', 'row'), may hold values from -1.5 to 1.5
- w_in: bfloat16 [12288, 24576], P('row', 'col'), may hold values from -0.0546875 to 0.0546875
- w_out: bfloat16 [24576, 12288], P('col', 'row'), may hold values from -0.0390625 to 0.0390625
Outputs:
- layer_out: bfloat16 [512, 12288], P('col', 'row')
- grad_tokens: bfloat16 [512, 12288], P('col', 'row')
- grad_w_in: bfloat16 [12288, 24576], P('row', 'col')
- grad_w_out: bfloat16 [24576, 12288], P('col', 'row')
The draws below stay inside these ranges and needn't reach their ends.
All inputs are finite; a program needn't handle non-finite values.
Results may differ from the reference program's by a relative error of at most 0.034.
Values may be sent and summed in bfloat16 or wider, within the bound.
A program may use at most 64 MiB of HBM per device.

```python
import jax
import jax.numpy as jnp
from jax import lax

D = 12288
FFW = 24576
TOKENS = 512
N_ROW = 32
N_COL = 16


def with_spikes(result, own_key, source, target, shards_of, factor):
    owner, partner = [(jnp.arange(result.shape[axis_at]) // (result.shape[axis_at] // shards_of)).reshape([-1 if axis == axis_at else 1 for axis in range(result.ndim)]) for axis_at in (source, target)]
    chosen = jax.random.permutation(own_key, shards_of)[partner]
    strong = (owner == chosen) | (owner == (partner + shards_of // 2) % shards_of)
    return jnp.where(strong, factor * result, result)


def shard_levels(own_key, shape, shards, low, high):
    factor_of = 1.0
    for dim, shards_of in shards:
        draws = jax.random.uniform(jax.random.fold_in(jax.random.fold_in(own_key, 6), dim), (shards_of,), jnp.float32, low / len(shards), high / len(shards))
        factor_of = factor_of * jnp.repeat(jnp.exp(draws), shape[dim] // shards_of).reshape((-1,) + (1,) * (len(shape) - 1 - dim))
    return factor_of


def noise(stream_key, dims, scale, reach, shards=(), kind=jnp.bfloat16):
    drawn = scale * jax.random.normal(stream_key, dims, jnp.float32)
    if shards:
        drawn = drawn * shard_levels(stream_key, dims, shards, -0.22, 0.18)
    return jnp.clip(drawn, -reach, reach).astype(kind)


def gaussian_with(key, extent, spread, reach, split, heavy, held_as=jnp.bfloat16):
    drawn = spread * jax.random.normal(key, extent, jnp.float32)
    if split:
        drawn = drawn * shard_levels(key, extent, split, -0.22, 0.18)
    return jnp.clip(with_spikes(drawn, jax.random.fold_in(key, 3), *heavy), -reach, reach).astype(held_as)


def setup_inputs(seed: int = 0) -> dict:
    key_of = jax.random.split(jax.random.key(seed), 5)
    return {
        "tokens": gaussian_with(key_of[0], (TOKENS, D), 1.0, 6.0, ((0, 16), (1, 32)), (1, 0, 32, 2.75)),
        "cotangent": gaussian_with(key_of[1], (TOKENS, D), 0.25, 1.5, ((0, 16), (1, 32)), (1, 0, 32, 2.75)),
        "w_in": noise(key_of[2], (D, FFW), D ** -0.5, 0.0546875, ((0, 32), (1, 16))),
        "w_out": noise(key_of[3], (FFW, D), FFW ** -0.5, 0.0390625, ((0, 16), (1, 32))),
    }


def gelu_fn(value):
    return jax.nn.gelu(value, approximate=True)

def block_sum(left, right, width, count):

    def step(total, index):
        start = (index * width).astype(jnp.int32)
        part_left = lax.dynamic_slice_in_dim(left, start, width, 1)
        part_right = lax.dynamic_slice_in_dim(right, start, width, 0)
        term = jnp.dot(part_left, part_right, preferred_element_type=jnp.float32).astype(jnp.bfloat16)
        term = lax.optimization_barrier(term)
        return (total + term.astype(jnp.float32), None)
    start_total = jnp.zeros((left.shape[0], right.shape[1]), jnp.float32)
    total, unused = lax.scan(step, start_total, jnp.arange(count, dtype=jnp.int32))
    return total

def reference(tokens, cotangent, w_in, w_out):
    width_block = D // N_ROW
    hidden_block = FFW // N_COL
    hidden = block_sum(tokens, w_in, width_block, N_ROW)
    act = gelu_fn(hidden).astype(jnp.bfloat16)
    layer_out = block_sum(act, w_out, hidden_block, N_COL).astype(jnp.bfloat16)
    grad_act = block_sum(cotangent, w_out.T, width_block, N_ROW)
    unused, pullback = jax.vjp(gelu_fn, hidden)
    grad_hidden = pullback(grad_act)[0].astype(jnp.bfloat16)
    grad_w_out = jnp.dot(act.T, cotangent, preferred_element_type=jnp.float32).astype(jnp.bfloat16)
    grad_w_in = jnp.dot(tokens.T, grad_hidden, preferred_element_type=jnp.float32).astype(jnp.bfloat16)
    grad_tokens = block_sum(grad_hidden, w_in.T, hidden_block, N_COL).astype(jnp.bfloat16)
    return (layer_out, grad_tokens, grad_w_in, grad_w_out)
```

```python
import functools
import math

import jax
import jax.numpy as jnp
from jax import lax
from jax.experimental import pallas as pl
from jax.experimental.pallas import tpu as pltpu
from jax.sharding import PartitionSpec as P

MESH = pl.DeviceIdType.MESH
BF16, F32 = jnp.bfloat16, jnp.float32
NZ = 16
CHUNK = 32
TOKENS = NZ * CHUNK
W = 384
CW = 2 * W
H = 1536
HH = H // 2
GROUPS = 2
ROWS = TOKENS // GROUPS
PART = ROWS // 4
PIECE = PART // 4
ORDER = [0, 15, 1, 14, 2, 13, 3, 12, 4, 11, 5, 10, 6, 9, 7, 8]
PLACE = {slot: place for place, slot in enumerate(ORDER)}
K0, K1 = math.sqrt(2.0 / math.pi), 0.044715


def chunk_rows(direction, steps):
    return pl.ds(PLACE[(-direction * steps) % NZ] * CHUNK, CHUNK)


def reach(which, direction):
    return 8 if (direction == 1) == (which == 0) else 7


def body(
    tokens, cotangent, w_in, w_out,
    layer_out, grad_tokens, grad_w_in, grad_w_out,
    ins, wi, wo, wi_pair, wo_pair, share, got1, mid, got2, full, part, zgot, zsum, outs, gwi, gwo,
    local_sem, send_sem, recv_sem,
):
    row, z = lax.axis_index("row"), lax.axis_index("col")
    x, y, c = row // 8, (row // 2) % 4, row % 2
    other = 1 - c
    own_cols = pl.ds(pl.multiple_of(c * W, 128), W)

    def along(axis, step):
        if axis == "x":
            return (((x + step) % 4) * 8 + y * 2 + c, z)
        if axis == "y":
            return (x * 8 + ((y + step) % 4) * 2 + c, z)
        return (row, (z + step + NZ) % NZ)

    pair = (x * 8 + y * 2 + other, z)
    at = {"x": x, "y": y}

    locals_, copies = [], {}

    def local(source, target):
        copy = pltpu.make_async_copy(source, target, local_sem.at[len(locals_)])
        copy.start()
        locals_.append(copy)
        return copy

    def send(key, source, target, device):
        index = len(copies)
        copies[key] = copy = pltpu.make_async_remote_copy(
            src_ref=source, dst_ref=target, send_sem=send_sem.at[index], recv_sem=recv_sem.at[index],
            device_id=device, device_id_type=MESH,
        )
        copy.start()

    def arrived(*key):
        copies[key].wait_recv()

    mine = [local(ref, ins.at[i, pl.ds(0, CHUNK), own_cols]) for i, ref in enumerate((tokens, cotangent))]
    barrier = pltpu.get_barrier_semaphore()
    partners = [along("x", s) for s in (1, 2, 3)] + [along("y", s) for s in (1, 2, 3)]
    partners += [along("z", s) for s in (-2, -1, 1, 2)] + [pair]
    for device in partners:
        pl.semaphore_signal(barrier, inc=1, device_id=device, device_id_type=MESH)
    own_weights = [
        local(w_in.at[:, pl.ds(pl.multiple_of(c * HH, 128), HH)], wi_pair.at[pl.ds(pl.multiple_of(c * W, 128), W)]),
        local(w_out.at[pl.ds(pl.multiple_of(c * HH, 128), HH)], wo_pair.at[:, own_cols]),
        local(w_in, wi),
        local(w_out, wo),
    ]
    pl.semaphore_wait(barrier, len(partners))
    for copy in mine:
        copy.wait()

    def pass_on(which, direction, steps):
        rows = chunk_rows(direction, steps)
        if steps % 2 == 0:
            for hop in (2, 1):
                if steps + hop <= reach(which, direction):
                    send(
                        ("gather", which, direction, steps + hop), ins.at[which, rows, own_cols],
                        ins.at[which, chunk_rows(direction, steps + hop), own_cols], along("z", direction * hop),
                    )

    def to_pair(which, direction, steps):
        rows = chunk_rows(direction, steps)
        key = ("pair", which, direction, steps)
        send(key, ins.at[which, rows, own_cols], ins.at[which, rows, own_cols], pair)

    def gather_step(steps):
        for which in range(2):
            for direction in (1, -1):
                if steps <= reach(which, direction):
                    arrived("gather", which, direction, steps)
                    pass_on(which, direction, steps)
                    to_pair(which, direction, steps)

    def pair_has(which, group):
        for place in range(8 * group, 8 * group + 8):
            slot = ORDER[place]
            if slot == 0:
                arrived("pair", which, 1, 0)
            elif slot == 8:
                arrived("pair", which, 1 if which == 0 else -1, 8)
            else:
                arrived("pair", which, *((-1, slot) if slot < 8 else (1, 16 - slot)))

    def group_rows(group, begin=0, count=ROWS):
        return pl.ds(group * ROWS + begin, count)

    def product(which, group):
        block = ins[which, group_rows(group), :]
        if which == 0:
            value = jnp.dot(block, wi_pair[...], preferred_element_type=F32)
        else:
            value = lax.dot_general(block, wo_pair[...], (((1,), (1,)), ((), ())), preferred_element_type=F32)
        share[which, group_rows(group), :] = value.astype(BF16)

    def axes(half):
        return ("x", "y") if half == 0 else ("y", "x")

    def cols(half):
        return pl.ds(half * W, W)

    def part_at(group, index):
        return pl.ds(pl.multiple_of(group * ROWS + index * PART, 16), PART)

    def piece_at(group, half):
        first, second = (at[a] for a in axes(half))
        return pl.ds(pl.multiple_of(group * ROWS + first * PART + second * PIECE, 16), PIECE)

    def scatter1(which, group):
        for step in (2, 1, 3):
            for half in range(2):
                axis = axes(half)[0]
                target = (at[axis] + step) % 4
                send(
                    ("s1", which, group, half, step), share.at[which, part_at(group, target), cols(half)],
                    got1.at[which, group, half, step - 1], along(axis, step),
                )

    def scatter2(which, group):
        for half in range(2):
            first, second = axes(half)
            total = share[which, part_at(group, at[first]), cols(half)].astype(F32)
            for step in (1, 3, 2):
                arrived("s1", which, group, half, step)
                total += got1[which, group, half, step - 1].astype(F32)
            mid[which, group, half] = total.astype(BF16)
            for step in (2, 1, 3):
                target = (at[second] + step) % 4
                send(
                    ("s2", which, group, half, step),
                    mid.at[which, group, half, pl.ds(pl.multiple_of(target * PIECE, 16), PIECE)],
                    got2.at[which, group, half, step - 1], along(second, step),
                )

    hidden = {}

    def finish(which, group):
        for half in range(2):
            second = axes(half)[1]
            total = mid[which, group, half, pl.ds(pl.multiple_of(at[second] * PIECE, 16), PIECE)].astype(F32)
            for step in (1, 3, 2):
                arrived("s2", which, group, half, step)
                total += got2[which, group, half, step - 1].astype(F32)
            if which == 0:
                hidden[group, half] = total
            v = hidden[group, half]
            t = jnp.tanh(K0 * (v + K1 * (v * v * v)))
            if which == 0:
                value = 0.5 * v * (1.0 + t)
            else:
                slope = 0.5 * (1.0 + t) + 0.5 * v * (1.0 - t * t) * (K0 * (1.0 + 3.0 * K1 * (v * v)))
                value = total * slope
            place = (which, c, piece_at(group, half), cols(half))
            full[place] = value.astype(BF16)
            for step in (2, 1, 3):
                send(("g1", which, group, half, step), full.at[place], full.at[place], along(second, step))

    def gather2(which, group):
        for half in range(2):
            first, second = axes(half)
            for step in (1, 3, 2):
                arrived("g1", which, group, half, step)
            place = (which, c, part_at(group, at[first]), cols(half))
            for step in (2, 1, 3):
                send(("g2", which, group, half, step), full.at[place], full.at[place], along(first, step))
            send(("gp", which, group, half, 0), full.at[place], full.at[place], pair)

    def gather3(which, group):
        for step in (1, 3, 2):
            for half in range(2):
                first = axes(half)[0]
                arrived("g2", which, group, half, step)
                place = (which, c, part_at(group, (at[first] + 4 - step) % 4), cols(half))
                send(("gp", which, group, half, step), full.at[place], full.at[place], pair)

    def project(which, group):
        for half in range(2):
            for step in range(4):
                arrived("gp", which, group, half, step)
        value = None
        for k in range(2):
            block = full[which, k, group_rows(group), :]
            if which == 0:
                term = jnp.dot(block, wo[pl.ds(k * HH, HH), :], preferred_element_type=F32)
            else:
                term = lax.dot_general(
                    block, wi[:, pl.ds(k * HH, HH)], (((1,), (1,)), ((), ())), preferred_element_type=F32
                )
            value = term if value is None else value + term
        part[which, group_rows(group), :] = value.astype(BF16)

    def zsend(which, direction, steps, source):
        hop = 1 if steps % 2 else 2
        send(
            ("z", which, direction, steps), source,
            zgot.at[which, 0 if direction == 1 else 1, (steps - hop) // 2, hop - 1], along("z", -direction * hop),
        )

    def zraw(which, group):
        for direction in (1, -1):
            for steps in (8, 7, 5, 3, 1):
                slot = (-direction * steps) % NZ
                if steps <= reach(which, direction) and PLACE[slot] // 8 == group:
                    zsend(which, direction, steps, part.at[which, chunk_rows(direction, steps)])

    def zadd(which, direction, steps, total):
        for hop in (1, 2):
            if steps + hop <= reach(which, direction):
                arrived("z", which, direction, steps + hop)
                total += zgot[which, 0 if direction == 1 else 1, steps // 2, hop - 1].astype(F32)
        return total

    def zstep(which, steps):
        for side, direction in enumerate((1, -1)):
            total = part[which, chunk_rows(direction, steps), :].astype(F32)
            zsum[which, side, steps // 2 - 1] = zadd(which, direction, steps, total).astype(BF16)
            zsend(which, direction, steps, zsum.at[which, side, steps // 2 - 1])

    def zend(which):
        total = part[which, chunk_rows(1, 0), :].astype(F32)
        for direction in (1, -1):
            total = zadd(which, direction, 0, total)
        outs[which] = total.astype(BF16)
        return local(outs.at[which], (layer_out, grad_tokens)[which])

    def weight_grad(which):
        own = ins[1 - which, :, own_cols]
        for k in range(2):
            if which == 0:
                value = lax.dot_general(full[0, k], own, (((0,), (0,)), ((), ())), preferred_element_type=F32)
                gwo[pl.ds(k * HH, HH), :] = value.astype(BF16)
            else:
                value = lax.dot_general(own, full[1, k], (((0,), (0,)), ((), ())), preferred_element_type=F32)
                gwi[:, pl.ds(k * HH, HH)] = value.astype(BF16)
        return local(gwo, grad_w_out) if which == 0 else local(gwi, grad_w_in)

    for hop in (2, 1):
        for which in range(2):
            for direction in (1, -1):
                send(
                    ("gather", which, direction, hop), ins.at[which, chunk_rows(1, 0), own_cols],
                    ins.at[which, chunk_rows(direction, hop), own_cols], along("z", direction * hop),
                )
    for which in range(2):
        to_pair(which, 1, 0)
    own_half, other_half = (pl.ds(pl.multiple_of(i * HH, 128), HH) for i in (c, other))
    send(("w", 0), w_in.at[:, other_half], wi_pair.at[pl.ds(pl.multiple_of(c * W, 128), W)], pair)
    send(("w", 1), w_out.at[other_half], wo_pair.at[:, own_cols], pair)

    for steps in (2, 1, 4, 3):
        gather_step(steps)
    for copy in own_weights:
        copy.wait()
    arrived("w", 0)
    pair_has(0, 0)
    product(0, 0)
    scatter1(0, 0)
    gather_step(6)
    arrived("w", 1)
    pair_has(1, 0)
    product(1, 0)
    scatter1(1, 0)
    gather_step(5)
    gather_step(8)
    gather_step(7)
    scatter2(0, 0)
    pair_has(0, 1)
    product(0, 1)
    scatter1(0, 1)
    scatter2(1, 0)
    pair_has(1, 1)
    product(1, 1)
    scatter1(1, 1)
    finish(0, 0)
    finish(1, 0)
    scatter2(0, 1)
    gather2(0, 0)
    scatter2(1, 1)
    gather2(1, 0)
    finish(0, 1)
    finish(1, 1)
    gather3(0, 0)
    gather2(0, 1)
    gather2(1, 1)
    gather3(1, 0)
    project(0, 0)
    zraw(0, 0)
    gather3(0, 1)
    project(1, 0)
    zraw(1, 0)
    project(0, 1)
    zraw(0, 1)
    gather3(1, 1)
    project(1, 1)
    zraw(1, 1)
    zstep(0, 6)
    zstep(1, 6)
    last = [weight_grad(0)]
    zstep(0, 4)
    zstep(1, 4)
    last.append(weight_grad(1))
    zstep(0, 2)
    zstep(1, 2)
    last.append(zend(0))
    last.append(zend(1))
    for copy in copies.values():
        copy.wait_send()
    for copy in last:
        copy.wait()


def shards(tokens, cotangent, w_in, w_out):
    copies = 2 * 15 + 2 * 16 + 2 + 4 * 6 * 4 + 4 * 8 + 2 * 15
    anywhere = pl.BlockSpec(memory_space=pl.ANY)
    shape = jax.ShapeDtypeStruct
    return pl.pallas_call(
        body,
        out_shape=(
            shape((CHUNK, W), BF16), shape((CHUNK, W), BF16), shape((W, H), BF16), shape((H, W), BF16),
        ),
        in_specs=[anywhere] * 4,
        out_specs=(anywhere,) * 4,
        scratch_shapes=[
            pltpu.VMEM((2, TOKENS, CW), BF16),
            pltpu.VMEM((W, H), BF16),
            pltpu.VMEM((H, W), BF16),
            pltpu.VMEM((CW, HH), BF16),
            pltpu.VMEM((HH, CW), BF16),
            pltpu.VMEM((2, TOKENS, HH), BF16),
            pltpu.VMEM((2, GROUPS, 2, 3, PART, W), BF16),
            pltpu.VMEM((2, GROUPS, 2, PART, W), BF16),
            pltpu.VMEM((2, GROUPS, 2, 3, PIECE, W), BF16),
            pltpu.VMEM((2, 2, TOKENS, HH), BF16),
            pltpu.VMEM((2, TOKENS, W), BF16),
            pltpu.VMEM((2, 2, 4, 2, CHUNK, W), BF16),
            pltpu.VMEM((2, 2, 3, CHUNK, W), BF16),
            pltpu.VMEM((2, CHUNK, W), BF16),
            pltpu.VMEM((W, H), BF16),
            pltpu.VMEM((H, W), BF16),
            pltpu.SemaphoreType.DMA((10,)),
            pltpu.SemaphoreType.DMA((copies,)),
            pltpu.SemaphoreType.DMA((copies,)),
        ],
        compiler_params=pltpu.CompilerParams(
            collective_id=0, has_side_effects=True, vmem_limit_bytes=48 * 2**20
        ),
        cost_estimate=pl.CostEstimate(flops=12 * TOKENS * W * H, bytes_accessed=10 * W * H, transcendentals=0),
        name="ffn",
    )(tokens, cotangent, w_in, w_out)


def solution(mesh):
    return jax.shard_map(
        shards,
        mesh=mesh,
        in_specs=(P("col", "row"), P("col", "row"), P("row", "col"), P("col", "row")),
        out_specs=(P("col", "row"), P("col", "row"), P("row", "col"), P("col", "row")),
        check_vma=False,
    )
```

```python
import functools
import math

import jax
import jax.numpy as jnp
from jax import lax
from jax.experimental import pallas as pl
from jax.experimental.pallas import tpu as pltpu
from jax.sharding import PartitionSpec as P

MESH = pl.DeviceIdType.MESH
BF16, F32 = jnp.bfloat16, jnp.float32
NZ = 16
CHUNK = 32
TOKENS = NZ * CHUNK
W = 384
CW = 2 * W
H = 1536
HH = H // 2
GROUPS = 2
SPAN = NZ // GROUPS
ROWS = TOKENS // GROUPS
PART = ROWS // 4
PIECE = PART // 4
ORDER = [0, 15, 1, 14, 2, 13, 3, 12, 4, 11, 5, 10, 6, 9, 7, 8]
PLACE = {slot: place for place, slot in enumerate(ORDER)}
GO_ON = {1: 0, 2: 0, 3: 2, 4: 2, 5: 4, 6: 4, 7: 6, 8: 6}
BEFORE = {1: 0, 2: 0, 3: 0, 4: 3, 5: 3, 6: 3, 7: 6, 8: 6}
FIRST = [steps for steps in (3, 2, 1) if GO_ON[steps] == 0]
K0, K1 = math.sqrt(2.0 / math.pi), 0.044715


def chunk_rows(direction, steps):
    return pl.ds(PLACE[(-direction * steps) % NZ] * CHUNK, CHUNK)


def reach(which, direction):
    return 8 if (direction == 1) == (which == 0) else 7


def body(
    tokens, cotangent, w_in, w_out,
    layer_out, grad_tokens, grad_w_in, grad_w_out,
    ins, wi, wo, wi_pair, wo_pair, share, got1, mid, got2, full, part, zgot, zsum, outs, gwi, gwo,
    local_sem, send_sem, recv_sem,
):
    row, z = lax.axis_index("row"), lax.axis_index("col")
    x, y, c = row // 8, (row // 2) % 4, row % 2
    other = 1 - c
    own_cols = pl.ds(pl.multiple_of(c * W, 128), W)

    def along(axis, step):
        if axis == "x":
            return (((x + step) % 4) * 8 + y * 2 + c, z)
        if axis == "y":
            return (x * 8 + ((y + step) % 4) * 2 + c, z)
        return (row, (z + step + NZ) % NZ)

    pair = (x * 8 + y * 2 + other, z)
    at = {"x": x, "y": y}

    locals_, copies = [], {}

    def local(source, target):
        copy = pltpu.make_async_copy(source, target, local_sem.at[len(locals_)])
        copy.start()
        locals_.append(copy)
        return copy

    def send(key, source, target, device):
        index = len(copies)
        copies[key] = copy = pltpu.make_async_remote_copy(
            src_ref=source, dst_ref=target, send_sem=send_sem.at[index], recv_sem=recv_sem.at[index],
            device_id=device, device_id_type=MESH,
        )
        copy.start()

    def arrived(*key):
        copies[key].wait_recv()

    gone = set()

    def sent():
        for key, copy in copies.items():
            if key not in gone:
                copy.wait_send()
                gone.add(key)

    mine = [local(ref, ins.at[i, pl.ds(0, CHUNK), own_cols]) for i, ref in enumerate((tokens, cotangent))]
    barrier = pltpu.get_barrier_semaphore()
    partners = [along("x", s) for s in (1, 2, 3)] + [along("y", s) for s in (1, 2, 3)]
    partners += [along("z", s) for s in (-3, -2, -1, 1, 2, 3)] + [pair]
    for device in partners:
        pl.semaphore_signal(barrier, inc=1, device_id=device, device_id_type=MESH)
    pl.semaphore_wait(barrier, len(partners))
    for copy in mine:
        copy.wait()

    def pass_on(which, steps):
        for direction in (1, -1):
            if steps <= reach(which, direction):
                source, hop = GO_ON[steps], steps - GO_ON[steps]
                send(
                    ("gather", which, direction, steps), ins.at[which, chunk_rows(direction, source), own_cols],
                    ins.at[which, chunk_rows(direction, steps), own_cols], along("z", direction * hop),
                )

    def to_pair(which, direction, steps):
        rows = chunk_rows(direction, steps)
        key = ("pair", which, direction, steps)
        send(key, ins.at[which, rows, own_cols], ins.at[which, rows, own_cols], pair)

    def chunk_in(which, *many):
        for steps in many:
            for direction in (1, -1):
                if steps <= reach(which, direction):
                    arrived("gather", which, direction, steps)

    def share_in(which, *many):
        for steps in many:
            for direction in (1, -1):
                if steps <= reach(which, direction):
                    to_pair(which, direction, steps)

    def pair_has(which, group):
        for place in range(SPAN * group, SPAN * group + SPAN):
            slot = ORDER[place]
            if slot == 0:
                arrived("pair", which, 1, 0)
            elif slot == 8:
                arrived("pair", which, 1 if which == 0 else -1, 8)
            else:
                arrived("pair", which, *((-1, slot) if slot < 8 else (1, 16 - slot)))

    def group_rows(group, begin=0, count=ROWS):
        return pl.ds(group * ROWS + begin, count)

    def product(which, group):
        block = ins[which, group_rows(group), :]
        if which == 0:
            value = jnp.dot(block, wi_pair[...], preferred_element_type=F32)
        else:
            value = lax.dot_general(block, wo_pair[...], (((1,), (1,)), ((), ())), preferred_element_type=F32)
        share[which, group_rows(group), :] = value.astype(BF16)

    def axes(half):
        return ("x", "y") if half == 0 else ("y", "x")

    def cols(half):
        return pl.ds(half * W, W)

    def part_at(group, index):
        return pl.ds(pl.multiple_of(group * ROWS + index * PART, 16), PART)

    def piece_at(group, half):
        first, second = (at[a] for a in axes(half))
        return pl.ds(pl.multiple_of(group * ROWS + first * PART + second * PIECE, 16), PIECE)

    def scatter1(which, group):
        for step in (2, 1, 3):
            for half in range(2):
                axis = axes(half)[0]
                target = (at[axis] + step) % 4
                send(
                    ("s1", which, group, half, step), share.at[which, part_at(group, target), cols(half)],
                    got1.at[which, group, half, step - 1], along(axis, step),
                )

    def scatter2(which, group):
        for half in range(2):
            first, second = axes(half)
            total = share[which, part_at(group, at[first]), cols(half)].astype(F32)
            for step in (1, 3, 2):
                arrived("s1", which, group, half, step)
                total += got1[which, group, half, step - 1].astype(F32)
            mid[which, group, half] = total.astype(BF16)
            for step in (2, 1, 3):
                target = (at[second] + step) % 4
                send(
                    ("s2", which, group, half, step),
                    mid.at[which, group, half, pl.ds(pl.multiple_of(target * PIECE, 16), PIECE)],
                    got2.at[which, group, half, step - 1], along(second, step),
                )

    hidden = {}

    def finish(which, group):
        for half in range(2):
            second = axes(half)[1]
            total = mid[which, group, half, pl.ds(pl.multiple_of(at[second] * PIECE, 16), PIECE)].astype(F32)
            for step in (1, 3, 2):
                arrived("s2", which, group, half, step)
                total += got2[which, group, half, step - 1].astype(F32)
            if which == 0:
                hidden[group, half] = total
            v = hidden[group, half]
            t = jnp.tanh(K0 * (v + K1 * (v * v * v)))
            if which == 0:
                value = 0.5 * v * (1.0 + t)
            else:
                slope = 0.5 * (1.0 + t) + 0.5 * v * (1.0 - t * t) * (K0 * (1.0 + 3.0 * K1 * (v * v)))
                value = total * slope
            place = (which, c, piece_at(group, half), cols(half))
            full[place] = value.astype(BF16)
            for step in (2, 1, 3):
                send(("g1", which, group, half, step), full.at[place], full.at[place], along(second, step))

    def gather2(which, group):
        for half in range(2):
            first, second = axes(half)
            for step in (1, 3, 2):
                arrived("g1", which, group, half, step)
            place = (which, c, part_at(group, at[first]), cols(half))
            for step in (2, 1, 3):
                send(("g2", which, group, half, step), full.at[place], full.at[place], along(first, step))
            send(("gp", which, group, half, 0), full.at[place], full.at[place], pair)

    def gather3(which, group):
        for step in (1, 3, 2):
            for half in range(2):
                first = axes(half)[0]
                arrived("g2", which, group, half, step)
                place = (which, c, part_at(group, (at[first] + 4 - step) % 4), cols(half))
                send(("gp", which, group, half, step), full.at[place], full.at[place], pair)

    def project(which, group):
        for half in range(2):
            for step in range(4):
                arrived("gp", which, group, half, step)
        value = None
        for k in range(2):
            block = full[which, k, group_rows(group), :]
            if which == 0:
                term = jnp.dot(block, wo[pl.ds(k * HH, HH), :], preferred_element_type=F32)
            else:
                term = lax.dot_general(
                    block, wi[:, pl.ds(k * HH, HH)], (((1,), (1,)), ((), ())), preferred_element_type=F32
                )
            value = term if value is None else value + term
        part[which, group_rows(group), :] = value.astype(BF16)

    def zsend(which, direction, steps, source):
        after = BEFORE[steps]
        send(
            ("z", which, direction, steps), source,
            zgot.at[which, 0 if direction == 1 else 1, after // 3, steps - after - 1],
            along("z", -direction * (steps - after)),
        )

    def zraw(which, group):
        for steps in (8, 7, 5, 4, 2, 1):
            for direction in (1, -1):
                slot = (-direction * steps) % NZ
                if steps <= reach(which, direction) and PLACE[slot] // SPAN == group:
                    zsend(which, direction, steps, part.at[which, chunk_rows(direction, steps)])

    def zadd(which, direction, steps, total):
        for source in (steps + 1, steps + 2, steps + 3):
            if source <= reach(which, direction) and BEFORE[source] == steps:
                arrived("z", which, direction, source)
                total += zgot[which, 0 if direction == 1 else 1, steps // 3, source - steps - 1].astype(F32)
        return total

    def zstep(which, steps):
        for side, direction in enumerate((1, -1)):
            total = part[which, chunk_rows(direction, steps), :].astype(F32)
            zsum[which, side, steps // 3 - 1] = zadd(which, direction, steps, total).astype(BF16)
            zsend(which, direction, steps, zsum.at[which, side, steps // 3 - 1])

    def zend(which):
        total = part[which, chunk_rows(1, 0), :].astype(F32)
        for direction in (1, -1):
            total = zadd(which, direction, 0, total)
        outs[which] = total.astype(BF16)
        return local(outs.at[which], (layer_out, grad_tokens)[which])

    def weight_grad(which):
        own = ins[1 - which, :, own_cols]
        for k in range(2):
            if which == 0:
                value = lax.dot_general(full[0, k], own, (((0,), (0,)), ((), ())), preferred_element_type=F32)
                gwo[pl.ds(k * HH, HH), :] = value.astype(BF16)
            else:
                value = lax.dot_general(own, full[1, k], (((0,), (0,)), ((), ())), preferred_element_type=F32)
                gwi[:, pl.ds(k * HH, HH)] = value.astype(BF16)
        return local(gwo, grad_w_out) if which == 0 else local(gwi, grad_w_in)

    for steps in FIRST:
        pass_on(0, steps)
        pass_on(1, steps)
    to_pair(0, 1, 0)
    to_pair(1, 1, 0)
    own_half, other_half = (pl.ds(pl.multiple_of(i * HH, 128), HH) for i in (c, other))
    send(("w", 0), w_in.at[:, other_half], wi_pair.at[pl.ds(pl.multiple_of(c * W, 128), W)], pair)
    send(("w", 1), w_out.at[other_half], wo_pair.at[:, own_cols], pair)

    own_weights = [
        local(w_in.at[:, own_half], wi_pair.at[pl.ds(pl.multiple_of(c * W, 128), W)]),
        local(w_out.at[own_half], wo_pair.at[:, own_cols]),
    ]
    last = []
    chunk_in(0, 2)
    pass_on(0, 4)
    chunk_in(1, 2)
    pass_on(1, 4)
    pass_on(0, 3)
    pass_on(1, 3)
    share_in(0, 2)
    share_in(1, 2)
    chunk_in(0, 1)
    share_in(0, 1)
    chunk_in(1, 1)
    share_in(1, 1)
    chunk_in(0, 4)
    pass_on(0, 6)
    chunk_in(1, 4)
    pass_on(1, 6)
    pass_on(0, 5)
    pass_on(1, 5)
    share_in(0, 4)
    share_in(1, 4)
    chunk_in(0, 3)
    share_in(0, 3)
    chunk_in(1, 3)
    share_in(1, 3)
    for copy in own_weights:
        copy.wait()
    arrived("w", 0)
    pair_has(0, 0)
    product(0, 0)
    scatter1(0, 0)
    chunk_in(0, 6)
    pass_on(0, 8)
    chunk_in(1, 6)
    pass_on(1, 8)
    pass_on(0, 7)
    pass_on(1, 7)
    share_in(0, 6)
    share_in(1, 6)
    arrived("w", 1)
    full_weights = [local(w_in, wi), local(w_out, wo)]
    pair_has(1, 0)
    product(1, 0)
    scatter1(1, 0)
    chunk_in(0, 5)
    share_in(0, 5)
    chunk_in(1, 5)
    share_in(1, 5)
    chunk_in(0, 8)
    share_in(0, 8)
    chunk_in(1, 8)
    share_in(1, 8)
    chunk_in(0, 7)
    share_in(0, 7)
    chunk_in(1, 7)
    share_in(1, 7)
    scatter2(0, 0)
    pair_has(0, 1)
    product(0, 1)
    scatter1(0, 1)
    scatter2(1, 0)
    pair_has(1, 1)
    product(1, 1)
    scatter1(1, 1)
    finish(0, 0)
    scatter2(0, 1)
    finish(1, 0)
    scatter2(1, 1)
    finish(0, 1)
    gather2(0, 0)
    finish(1, 1)
    gather2(0, 1)
    gather2(1, 0)
    gather2(1, 1)
    gather3(0, 0)
    for copy in full_weights:
        copy.wait()
    project(0, 0)
    zraw(0, 0)
    gather3(0, 1)
    project(0, 1)
    zraw(0, 1)
    last.append(weight_grad(0))
    gather3(1, 0)
    project(1, 0)
    zraw(1, 0)
    gather3(1, 1)
    zstep(0, 6)
    project(1, 1)
    zraw(1, 1)
    sent()
    zstep(1, 6)
    zstep(0, 3)
    last.append(weight_grad(1))
    zstep(1, 3)
    sent()
    last.append(zend(0))
    last.append(zend(1))
    sent()
    for copy in last:
        copy.wait()


def to_outputs(*refs):
    sources, targets, held, sems = refs[:4], refs[4:8], refs[8:12], refs[12]
    blocks = [(i, pl.ds(k * held[i].shape[0] // 4, held[i].shape[0] // 4)) for k in range(4) for i in (2, 3)]
    blocks += [(0, pl.ds(0, CHUNK)), (1, pl.ds(0, CHUNK))]
    first = [pltpu.make_async_copy(sources[i].at[r], held[i].at[r], sems.at[0, n]) for n, (i, r) in enumerate(blocks)]
    second = [pltpu.make_async_copy(held[i].at[r], targets[i].at[r], sems.at[1, n]) for n, (i, r) in enumerate(blocks)]
    for copy in first:
        copy.start()
    for before, after in zip(first, second):
        before.wait()
        after.start()
    for copy in second:
        copy.wait()


def shards(tokens, cotangent, w_in, w_out):
    results = kernel_call(tokens, cotangent, w_in, w_out)
    return pl.pallas_call(
        to_outputs,
        out_shape=tuple(jax.ShapeDtypeStruct(r.shape, r.dtype) for r in results),
        in_specs=[pl.BlockSpec(memory_space=pl.ANY)] * 4,
        out_specs=(pl.BlockSpec(memory_space=pl.ANY),) * 4,
        scratch_shapes=[*(pltpu.VMEM(r.shape, r.dtype) for r in results), pltpu.SemaphoreType.DMA((2, 10))],
        name="to_outputs",
    )(*results)


def kernel_call(tokens, cotangent, w_in, w_out):
    copies = 2 * 15 + 2 * 16 + 2 + 2 * GROUPS * 32 + 2 * 15
    anywhere = pl.BlockSpec(memory_space=pl.ANY)
    shape = jax.ShapeDtypeStruct
    return pl.pallas_call(
        body,
        out_shape=(
            shape((CHUNK, W), BF16), shape((CHUNK, W), BF16), shape((W, H), BF16), shape((H, W), BF16),
        ),
        in_specs=[pl.BlockSpec(memory_space=pltpu.HBM)] * 4,
        out_specs=(anywhere,) * 4,
        scratch_shapes=[
            pltpu.VMEM((2, TOKENS, CW), BF16),
            pltpu.VMEM((W, H), BF16),
            pltpu.VMEM((H, W), BF16),
            pltpu.VMEM((CW, HH), BF16),
            pltpu.VMEM((HH, CW), BF16),
            pltpu.VMEM((2, TOKENS, HH), BF16),
            pltpu.VMEM((2, GROUPS, 2, 3, PART, W), BF16),
            pltpu.VMEM((2, GROUPS, 2, PART, W), BF16),
            pltpu.VMEM((2, GROUPS, 2, 3, PIECE, W), BF16),
            pltpu.VMEM((2, 2, TOKENS, HH), BF16),
            pltpu.VMEM((2, TOKENS, W), BF16),
            pltpu.VMEM((2, 2, 3, 3, CHUNK, W), BF16),
            pltpu.VMEM((2, 2, 2, CHUNK, W), BF16),
            pltpu.VMEM((2, CHUNK, W), BF16),
            pltpu.VMEM((W, H), BF16),
            pltpu.VMEM((H, W), BF16),
            pltpu.SemaphoreType.DMA((10,)),
            pltpu.SemaphoreType.DMA((copies,)),
            pltpu.SemaphoreType.DMA((copies,)),
        ],
        compiler_params=pltpu.CompilerParams(
            collective_id=0, has_side_effects=True, vmem_limit_bytes=60 * 2**20
        ),
        cost_estimate=pl.CostEstimate(flops=12 * TOKENS * W * H, bytes_accessed=10 * W * H, transcendentals=0),
        name="ffn",
    )(tokens, cotangent, w_in, w_out)


def solution(mesh):
    return jax.shard_map(
        shards,
        mesh=mesh,
        in_specs=(P("col", "row"), P("col", "row"), P("row", "col"), P("col", "row")),
        out_specs=(P("col", "row"), P("col", "row"), P("row", "col"), P("col", "row")),
        check_vma=False,
    )
```

```python
import functools
import math

import jax
import jax.numpy as jnp
from jax import lax
from jax.experimental import pallas as pl
from jax.experimental.pallas import tpu as pltpu
from jax.sharding import PartitionSpec as P

MESH = pl.DeviceIdType.MESH
BF16, F32 = jnp.bfloat16, jnp.float32
NZ = 16
CHUNK = 32
TOKENS = NZ * CHUNK
W = 384
CW = 2 * W
H = 1536
HH = H // 2
GROUPS = 2
SPAN = NZ // GROUPS
ROWS = TOKENS // GROUPS
PART = ROWS // 4
PIECE = PART // 4
ORDER = [0, 15, 1, 14, 2, 13, 3, 12, 4, 11, 5, 10, 6, 9, 7, 8]
PLACE = {slot: place for place, slot in enumerate(ORDER)}
GO_ON = {1: 0, 2: 0, 3: 2, 4: 2, 5: 4, 6: 4, 7: 6, 8: 6}
BEFORE = {1: 0, 2: 0, 3: 0, 4: 3, 5: 3, 6: 3, 7: 6, 8: 6}
FIRST = [steps for steps in (3, 2, 1) if GO_ON[steps] == 0]
K0, K1 = math.sqrt(2.0 / math.pi), 0.044715


def chunk_rows(direction, steps):
    return pl.ds(PLACE[(-direction * steps) % NZ] * CHUNK, CHUNK)


def reach(which, direction):
    return 8 if (direction == 1) == (which == 0) else 7


def body(
    tokens, cotangent, w_in, w_out,
    layer_out, grad_tokens, grad_w_in, grad_w_out,
    ins, wi, wo, wi_pair, wo_pair, share, got1, mid, got2, full, part, zgot, zsum, outs, gwi, gwo,
    local_sem, send_sem, recv_sem,
):
    row, z = lax.axis_index("row"), lax.axis_index("col")
    x, y, c = row // 8, (row // 2) % 4, row % 2
    other = 1 - c
    own_cols = pl.ds(pl.multiple_of(c * W, 128), W)

    def along(axis, step):
        if axis == "x":
            return (((x + step) % 4) * 8 + y * 2 + c, z)
        if axis == "y":
            return (x * 8 + ((y + step) % 4) * 2 + c, z)
        return (row, (z + step + NZ) % NZ)

    pair = (x * 8 + y * 2 + other, z)
    at = {"x": x, "y": y}

    locals_, copies = [], {}

    def local(source, target):
        copy = pltpu.make_async_copy(source, target, local_sem.at[len(locals_)])
        copy.start()
        locals_.append(copy)
        return copy

    def send(key, source, target, device):
        index = len(copies)
        copies[key] = copy = pltpu.make_async_remote_copy(
            src_ref=source, dst_ref=target, send_sem=send_sem.at[index], recv_sem=recv_sem.at[index],
            device_id=device, device_id_type=MESH,
        )
        copy.start()

    def arrived(*key):
        copies[key].wait_recv()

    gone = set()

    def sent():
        for key, copy in copies.items():
            if key not in gone:
                copy.wait_send()
                gone.add(key)

    mine = [local(ref, ins.at[i, pl.ds(0, CHUNK), own_cols]) for i, ref in enumerate((tokens, cotangent))]
    barrier = pltpu.get_barrier_semaphore()
    partners = [along("x", s) for s in (1, 2, 3)] + [along("y", s) for s in (1, 2, 3)]
    partners += [along("z", s) for s in (-3, -2, -1, 1, 2, 3)] + [pair]
    for device in partners:
        pl.semaphore_signal(barrier, inc=1, device_id=device, device_id_type=MESH)
    pl.semaphore_wait(barrier, len(partners))
    for copy in mine:
        copy.wait()

    def pass_on(which, steps):
        for direction in (1, -1):
            if steps <= reach(which, direction):
                source, hop = GO_ON[steps], steps - GO_ON[steps]
                send(
                    ("gather", which, direction, steps), ins.at[which, chunk_rows(direction, source), own_cols],
                    ins.at[which, chunk_rows(direction, steps), own_cols], along("z", direction * hop),
                )

    def chunk_in(which, *many):
        for steps in many:
            for direction in (1, -1):
                if steps <= reach(which, direction):
                    arrived("gather", which, direction, steps)

    def group_rows(group, begin=0, count=ROWS):
        return pl.ds(group * ROWS + begin, count)

    def to_pair(which, group):
        place = (which, group_rows(group), own_cols)
        send(("pair", which, group), ins.at[place], ins.at[place], pair)

    def product(which, group):
        block = ins[which, group_rows(group), :]
        if which == 0:
            value = jnp.dot(block, wi_pair[...], preferred_element_type=F32)
        else:
            value = lax.dot_general(block, wo_pair[...], (((1,), (1,)), ((), ())), preferred_element_type=F32)
        share[which, group_rows(group), :] = value.astype(BF16)

    def axes(half):
        return ("x", "y") if half == 0 else ("y", "x")

    def cols(half):
        return pl.ds(half * W, W)

    def part_at(group, index):
        return pl.ds(pl.multiple_of(group * ROWS + index * PART, 16), PART)

    def piece_at(group, half):
        first, second = (at[a] for a in axes(half))
        return pl.ds(pl.multiple_of(group * ROWS + first * PART + second * PIECE, 16), PIECE)

    def scatter1(which, group):
        for step in (2, 1, 3):
            for half in range(2):
                axis = axes(half)[0]
                target = (at[axis] + step) % 4
                send(
                    ("s1", which, group, half, step), share.at[which, part_at(group, target), cols(half)],
                    got1.at[which, group, half, step - 1], along(axis, step),
                )

    def scatter2(which, group):
        for half in range(2):
            first, second = axes(half)
            total = share[which, part_at(group, at[first]), cols(half)].astype(F32)
            for step in (1, 3, 2):
                arrived("s1", which, group, half, step)
                total += got1[which, group, half, step - 1].astype(F32)
            mid[which, group, half] = total.astype(BF16)
            for step in (2, 1, 3):
                target = (at[second] + step) % 4
                send(
                    ("s2", which, group, half, step),
                    mid.at[which, group, half, pl.ds(pl.multiple_of(target * PIECE, 16), PIECE)],
                    got2.at[which, group, half, step - 1], along(second, step),
                )

    hidden = {}

    def finish(which, group):
        for half in range(2):
            second = axes(half)[1]
            total = mid[which, group, half, pl.ds(pl.multiple_of(at[second] * PIECE, 16), PIECE)].astype(F32)
            for step in (1, 3, 2):
                arrived("s2", which, group, half, step)
                total += got2[which, group, half, step - 1].astype(F32)
            if which == 0:
                hidden[group, half] = total
            v = hidden[group, half]
            t = jnp.tanh(K0 * (v + K1 * (v * v * v)))
            if which == 0:
                value = 0.5 * v * (1.0 + t)
            else:
                slope = 0.5 * (1.0 + t) + 0.5 * v * (1.0 - t * t) * (K0 * (1.0 + 3.0 * K1 * (v * v)))
                value = total * slope
            place = (which, c, piece_at(group, half), cols(half))
            full[place] = value.astype(BF16)
            for step in (2, 1, 3):
                send(("g1", which, group, half, step), full.at[place], full.at[place], along(second, step))

    def gather2(which, group):
        for half in range(2):
            first, second = axes(half)
            for step in (1, 3, 2):
                arrived("g1", which, group, half, step)
            place = (which, c, part_at(group, at[first]), cols(half))
            for step in (2, 1, 3):
                send(("g2", which, group, half, step), full.at[place], full.at[place], along(first, step))

    def gather3(which, group):
        for half in range(2):
            for step in (1, 3, 2):
                arrived("g2", which, group, half, step)
            place = (which, c, group_rows(group), cols(half))
            send(("gp", which, group, half), full.at[place], full.at[place], pair)

    def project(which, group):
        for half in range(2):
            arrived("gp", which, group, half)
        value = None
        for k in range(2):
            block = full[which, k, group_rows(group), :]
            if which == 0:
                term = jnp.dot(block, wo[pl.ds(k * HH, HH), :], preferred_element_type=F32)
            else:
                term = lax.dot_general(
                    block, wi[:, pl.ds(k * HH, HH)], (((1,), (1,)), ((), ())), preferred_element_type=F32
                )
            value = term if value is None else value + term
        part[which, group_rows(group), :] = value.astype(BF16)

    def zsend(which, direction, steps, source):
        after = BEFORE[steps]
        send(
            ("z", which, direction, steps), source,
            zgot.at[which, 0 if direction == 1 else 1, after // 3, steps - after - 1],
            along("z", -direction * (steps - after)),
        )

    def zraw(which, group):
        for steps in (8, 7, 5, 4, 2, 1):
            for direction in (1, -1):
                slot = (-direction * steps) % NZ
                if steps <= reach(which, direction) and PLACE[slot] // SPAN == group:
                    zsend(which, direction, steps, part.at[which, chunk_rows(direction, steps)])

    def zadd(which, direction, steps, total):
        for source in (steps + 1, steps + 2, steps + 3):
            if source <= reach(which, direction) and BEFORE[source] == steps:
                arrived("z", which, direction, source)
                total += zgot[which, 0 if direction == 1 else 1, steps // 3, source - steps - 1].astype(F32)
        return total

    def zstep(which, steps):
        for side, direction in enumerate((1, -1)):
            total = part[which, chunk_rows(direction, steps), :].astype(F32)
            zsum[which, side, steps // 3 - 1] = zadd(which, direction, steps, total).astype(BF16)
            zsend(which, direction, steps, zsum.at[which, side, steps // 3 - 1])

    def zend(which):
        total = part[which, chunk_rows(1, 0), :].astype(F32)
        for direction in (1, -1):
            total = zadd(which, direction, 0, total)
        outs[which] = total.astype(BF16)
        return local(outs.at[which], (layer_out, grad_tokens)[which])

    def weight_grad(which):
        own = ins[1 - which, :, own_cols]
        for k in range(2):
            if which == 0:
                value = lax.dot_general(full[0, k], own, (((0,), (0,)), ((), ())), preferred_element_type=F32)
                gwo[pl.ds(k * HH, HH), :] = value.astype(BF16)
            else:
                value = lax.dot_general(own, full[1, k], (((0,), (0,)), ((), ())), preferred_element_type=F32)
                gwi[:, pl.ds(k * HH, HH)] = value.astype(BF16)
        return local(gwo, grad_w_out) if which == 0 else local(gwi, grad_w_in)

    for steps in FIRST:
        pass_on(0, steps)
        pass_on(1, steps)
    own_half, other_half = (pl.ds(pl.multiple_of(i * HH, 128), HH) for i in (c, other))

    own_weights = [
        local(w_in.at[:, own_half], wi_pair.at[pl.ds(pl.multiple_of(c * W, 128), W)]),
        local(w_out.at[own_half], wo_pair.at[:, own_cols]),
    ]
    last = []
    chunk_in(0, 2)
    pass_on(0, 4)
    chunk_in(1, 2)
    pass_on(1, 4)
    pass_on(0, 3)
    pass_on(1, 3)
    send(("w", 0), w_in.at[:, other_half], wi_pair.at[pl.ds(pl.multiple_of(c * W, 128), W)], pair)
    send(("w", 1), w_out.at[other_half], wo_pair.at[:, own_cols], pair)
    chunk_in(0, 1)
    chunk_in(1, 1)
    chunk_in(0, 4)
    pass_on(0, 6)
    chunk_in(1, 4)
    pass_on(1, 6)
    pass_on(0, 5)
    pass_on(1, 5)
    chunk_in(0, 3)
    to_pair(0, 0)
    chunk_in(1, 3)
    to_pair(1, 0)
    for copy in own_weights:
        copy.wait()
    arrived("w", 0)
    arrived("pair", 0, 0)
    product(0, 0)
    scatter1(0, 0)
    chunk_in(0, 6)
    pass_on(0, 8)
    chunk_in(1, 6)
    pass_on(1, 8)
    pass_on(0, 7)
    pass_on(1, 7)
    arrived("w", 1)
    full_weights = [local(w_in, wi), local(w_out, wo)]
    arrived("pair", 1, 0)
    product(1, 0)
    scatter1(1, 0)
    chunk_in(0, 5)
    chunk_in(1, 5)
    chunk_in(0, 8)
    chunk_in(1, 8)
    chunk_in(0, 7)
    to_pair(0, 1)
    chunk_in(1, 7)
    to_pair(1, 1)
    scatter2(0, 0)
    arrived("pair", 0, 1)
    product(0, 1)
    scatter1(0, 1)
    scatter2(1, 0)
    arrived("pair", 1, 1)
    product(1, 1)
    scatter1(1, 1)
    finish(0, 0)
    scatter2(0, 1)
    finish(1, 0)
    scatter2(1, 1)
    finish(0, 1)
    gather2(0, 0)
    finish(1, 1)
    gather2(0, 1)
    gather2(1, 0)
    gather2(1, 1)
    gather3(0, 0)
    for copy in full_weights:
        copy.wait()
    project(0, 0)
    zraw(0, 0)
    gather3(0, 1)
    project(0, 1)
    zraw(0, 1)
    last.append(weight_grad(0))
    gather3(1, 0)
    project(1, 0)
    zraw(1, 0)
    gather3(1, 1)
    zstep(0, 6)
    project(1, 1)
    zraw(1, 1)
    zstep(1, 6)
    zstep(0, 3)
    sent()
    zstep(1, 3)
    last.append(weight_grad(1))
    last.append(zend(0))
    last.append(zend(1))
    sent()
    for copy in last:
        copy.wait()


def to_outputs(*refs):
    sources, targets, held, sems = refs[:4], refs[4:8], refs[8:12], refs[12]
    blocks = [(i, pl.ds(k * held[i].shape[0] // 4, held[i].shape[0] // 4)) for k in range(4) for i in (2, 3)]
    blocks += [(0, pl.ds(0, CHUNK)), (1, pl.ds(0, CHUNK))]
    first = [pltpu.make_async_copy(sources[i].at[r], held[i].at[r], sems.at[0, n]) for n, (i, r) in enumerate(blocks)]
    second = [pltpu.make_async_copy(held[i].at[r], targets[i].at[r], sems.at[1, n]) for n, (i, r) in enumerate(blocks)]
    for copy in first:
        copy.start()
    for before, after in zip(first, second):
        before.wait()
        after.start()
    for copy in second:
        copy.wait()


def shards(tokens, cotangent, w_in, w_out):
    results = kernel_call(tokens, cotangent, w_in, w_out)
    return pl.pallas_call(
        to_outputs,
        out_shape=tuple(jax.ShapeDtypeStruct(r.shape, r.dtype) for r in results),
        in_specs=[pl.BlockSpec(memory_space=pl.ANY)] * 4,
        out_specs=(pl.BlockSpec(memory_space=pl.ANY),) * 4,
        scratch_shapes=[*(pltpu.VMEM(r.shape, r.dtype) for r in results), pltpu.SemaphoreType.DMA((2, 10))],
        name="to_outputs",
    )(*results)


def kernel_call(tokens, cotangent, w_in, w_out):
    copies = 2 * 15 + 2 * GROUPS + 2 + 2 * GROUPS * 26 + 2 * 15
    anywhere = pl.BlockSpec(memory_space=pl.ANY)
    shape = jax.ShapeDtypeStruct
    return pl.pallas_call(
        body,
        out_shape=(
            shape((CHUNK, W), BF16), shape((CHUNK, W), BF16), shape((W, H), BF16), shape((H, W), BF16),
        ),
        in_specs=[pl.BlockSpec(memory_space=pltpu.HBM)] * 4,
        out_specs=(anywhere,) * 4,
        scratch_shapes=[
            pltpu.VMEM((2, TOKENS, CW), BF16),
            pltpu.VMEM((W, H), BF16),
            pltpu.VMEM((H, W), BF16),
            pltpu.VMEM((CW, HH), BF16),
            pltpu.VMEM((HH, CW), BF16),
            pltpu.VMEM((2, TOKENS, HH), BF16),
            pltpu.VMEM((2, GROUPS, 2, 3, PART, W), BF16),
            pltpu.VMEM((2, GROUPS, 2, PART, W), BF16),
            pltpu.VMEM((2, GROUPS, 2, 3, PIECE, W), BF16),
            pltpu.VMEM((2, 2, TOKENS, HH), BF16),
            pltpu.VMEM((2, TOKENS, W), BF16),
            pltpu.VMEM((2, 2, 3, 3, CHUNK, W), BF16),
            pltpu.VMEM((2, 2, 2, CHUNK, W), BF16),
            pltpu.VMEM((2, CHUNK, W), BF16),
            pltpu.VMEM((W, H), BF16),
            pltpu.VMEM((H, W), BF16),
            pltpu.SemaphoreType.DMA((10,)),
            pltpu.SemaphoreType.DMA((copies,)),
            pltpu.SemaphoreType.DMA((copies,)),
        ],
        compiler_params=pltpu.CompilerParams(
            collective_id=0, has_side_effects=True, vmem_limit_bytes=60 * 2**20
        ),
        cost_estimate=pl.CostEstimate(flops=12 * TOKENS * W * H, bytes_accessed=10 * W * H, transcendentals=0),
        name="ffn",
    )(tokens, cotangent, w_in, w_out)


def solution(mesh):
    return jax.shard_map(
        shards,
        mesh=mesh,
        in_specs=(P("col", "row"), P("col", "row"), P("row", "col"), P("col", "row")),
        out_specs=(P("col", "row"), P("col", "row"), P("row", "col"), P("col", "row")),
        check_vma=False,
    )
```

```python
import functools
import math

import jax
import jax.numpy as jnp
from jax import lax
from jax.experimental import pallas as pl
from jax.experimental.pallas import tpu as pltpu
from jax.sharding import PartitionSpec as P

MESH = pl.DeviceIdType.MESH
BF16, F32 = jnp.bfloat16, jnp.float32
NZ = 16
CHUNK = 32
TOKENS = NZ * CHUNK
W = 384
CW = 2 * W
H = 1536
HH = H // 2
GROUPS = 2
SPAN = NZ // GROUPS
ROWS = TOKENS // GROUPS
PART = ROWS // 4
PIECE = PART // 4
ORDER = [0, 15, 1, 14, 2, 13, 3, 12, 4, 11, 5, 10, 6, 9, 7, 8]
PLACE = {slot: place for place, slot in enumerate(ORDER)}
GO_ON = {1: 0, 2: 0, 3: 2, 4: 2, 5: 4, 6: 4, 7: 6, 8: 6}
BEFORE = {1: 0, 2: 0, 3: 0, 4: 3, 5: 3, 6: 3, 7: 6, 8: 6}
FIRST = [steps for steps in (3, 2, 1) if GO_ON[steps] == 0]
K0, K1 = math.sqrt(2.0 / math.pi), 0.044715


def chunk_rows(direction, steps):
    return pl.ds(PLACE[(-direction * steps) % NZ] * CHUNK, CHUNK)


def reach(which, direction):
    return 8 if (direction == 1) == (which == 0) else 7


def body(
    tokens, cotangent, w_in, w_out,
    layer_out, grad_tokens, grad_w_in, grad_w_out,
    ins, wi, wo, wi_pair, wo_pair, share, got1, mid, got2, full, part, zgot, zsum, outs, gwi, gwo,
    local_sem, send_sem, recv_sem,
):
    row, z = lax.axis_index("row"), lax.axis_index("col")
    x, y, c = row // 8, (row // 2) % 4, row % 2
    other = 1 - c
    own_cols = pl.ds(pl.multiple_of(c * W, 128), W)

    def along(axis, step):
        if axis == "x":
            return (((x + step) % 4) * 8 + y * 2 + c, z)
        if axis == "y":
            return (x * 8 + ((y + step) % 4) * 2 + c, z)
        return (row, (z + step + NZ) % NZ)

    pair = (x * 8 + y * 2 + other, z)
    at = {"x": x, "y": y}

    locals_, copies = [], {}

    def local(source, target):
        copy = pltpu.make_async_copy(source, target, local_sem.at[len(locals_)])
        copy.start()
        locals_.append(copy)
        return copy

    def send(key, source, target, device):
        index = len(copies)
        copies[key] = copy = pltpu.make_async_remote_copy(
            src_ref=source, dst_ref=target, send_sem=send_sem.at[index], recv_sem=recv_sem.at[index],
            device_id=device, device_id_type=MESH,
        )
        copy.start()

    def arrived(*key):
        copies[key].wait_recv()

    gone = set()

    def sent():
        for key, copy in copies.items():
            if key not in gone:
                copy.wait_send()
                gone.add(key)

    mine = [local(ref, ins.at[i, pl.ds(0, CHUNK), own_cols]) for i, ref in enumerate((tokens, cotangent))]
    barrier = pltpu.get_barrier_semaphore()
    partners = [along("x", s) for s in (1, 2, 3)] + [along("y", s) for s in (1, 2, 3)]
    partners += [along("z", s) for s in (-3, -2, -1, 1, 2, 3)] + [pair]
    for device in partners:
        pl.semaphore_signal(barrier, inc=1, device_id=device, device_id_type=MESH)
    pl.semaphore_wait(barrier, len(partners))
    for copy in mine:
        copy.wait()

    def pass_on(which, steps):
        for direction in (1, -1):
            if steps <= reach(which, direction):
                source, hop = GO_ON[steps], steps - GO_ON[steps]
                send(
                    ("gather", which, direction, steps), ins.at[which, chunk_rows(direction, source), own_cols],
                    ins.at[which, chunk_rows(direction, steps), own_cols], along("z", direction * hop),
                )

    def chunk_in(which, *many):
        for steps in many:
            for direction in (1, -1):
                if steps <= reach(which, direction):
                    arrived("gather", which, direction, steps)

    def group_rows(group, begin=0, count=ROWS):
        return pl.ds(group * ROWS + begin, count)

    def to_pair(which, group):
        place = (which, group_rows(group), own_cols)
        send(("pair", which, group), ins.at[place], ins.at[place], pair)

    def product(which, group):
        block = ins[which, group_rows(group), :]
        if which == 0:
            value = jnp.dot(block, wi_pair[...], preferred_element_type=F32)
        else:
            value = lax.dot_general(block, wo_pair[...], (((1,), (1,)), ((), ())), preferred_element_type=F32)
        share[which, group_rows(group), :] = value.astype(BF16)

    def axes(half):
        return ("x", "y") if half == 0 else ("y", "x")

    def cols(half):
        return pl.ds(half * W, W)

    def part_at(group, index):
        return pl.ds(pl.multiple_of(group * ROWS + index * PART, 16), PART)

    def piece_at(group, half):
        first, second = (at[a] for a in axes(half))
        return pl.ds(pl.multiple_of(group * ROWS + first * PART + second * PIECE, 16), PIECE)

    def scatter1(which, group):
        for step in (2, 1, 3):
            for half in range(2):
                axis = axes(half)[0]
                target = (at[axis] + step) % 4
                send(
                    ("s1", which, group, half, step), share.at[which, part_at(group, target), cols(half)],
                    got1.at[which, group, half, step - 1], along(axis, step),
                )

    def scatter2(which, group):
        for half in range(2):
            first, second = axes(half)
            total = share[which, part_at(group, at[first]), cols(half)].astype(F32)
            for step in (1, 3, 2):
                arrived("s1", which, group, half, step)
                total += got1[which, group, half, step - 1].astype(F32)
            mid[which, group, half] = total.astype(BF16)
            for step in (2, 1, 3):
                target = (at[second] + step) % 4
                send(
                    ("s2", which, group, half, step),
                    mid.at[which, group, half, pl.ds(pl.multiple_of(target * PIECE, 16), PIECE)],
                    got2.at[which, group, half, step - 1], along(second, step),
                )

    hidden = {}

    def finish(which, group):
        for half in range(2):
            second = axes(half)[1]
            total = mid[which, group, half, pl.ds(pl.multiple_of(at[second] * PIECE, 16), PIECE)].astype(F32)
            for step in (1, 3, 2):
                arrived("s2", which, group, half, step)
                total += got2[which, group, half, step - 1].astype(F32)
            if which == 0:
                hidden[group, half] = total
            v = hidden[group, half]
            t = jnp.tanh(K0 * (v + K1 * (v * v * v)))
            if which == 0:
                value = 0.5 * v * (1.0 + t)
            else:
                slope = 0.5 * (1.0 + t) + 0.5 * v * (1.0 - t * t) * (K0 * (1.0 + 3.0 * K1 * (v * v)))
                value = total * slope
            place = (which, c, piece_at(group, half), cols(half))
            full[place] = value.astype(BF16)
            for step in (2, 1, 3):
                send(("g1", which, group, half, step), full.at[place], full.at[place], along(second, step))

    def gather2(which, group):
        for half in range(2):
            first, second = axes(half)
            for step in (1, 3, 2):
                arrived("g1", which, group, half, step)
            place = (which, c, part_at(group, at[first]), cols(half))
            for step in (2, 1, 3):
                send(("g2", which, group, half, step), full.at[place], full.at[place], along(first, step))

    def gather3(which, group):
        for half in range(2):
            for step in (1, 3, 2):
                arrived("g2", which, group, half, step)
            place = (which, c, group_rows(group), cols(half))
            send(("gp", which, group, half), full.at[place], full.at[place], pair)

    def project(which, group):
        for half in range(2):
            arrived("gp", which, group, half)
        value = None
        for k in range(2):
            block = full[which, k, group_rows(group), :]
            if which == 0:
                term = jnp.dot(block, wo[pl.ds(k * HH, HH), :], preferred_element_type=F32)
            else:
                term = lax.dot_general(
                    block, wi[:, pl.ds(k * HH, HH)], (((1,), (1,)), ((), ())), preferred_element_type=F32
                )
            value = term if value is None else value + term
        part[which, group_rows(group), :] = value.astype(BF16)

    def zsend(which, direction, steps, source):
        after = BEFORE[steps]
        send(
            ("z", which, direction, steps), source,
            zgot.at[which, 0 if direction == 1 else 1, after // 3, steps - after - 1],
            along("z", -direction * (steps - after)),
        )

    def zraw(which, group):
        for steps in (8, 7, 5, 4, 2, 1):
            for direction in (1, -1):
                slot = (-direction * steps) % NZ
                if steps <= reach(which, direction) and PLACE[slot] // SPAN == group:
                    zsend(which, direction, steps, part.at[which, chunk_rows(direction, steps)])

    def zadd(which, direction, steps, total):
        for source in (steps + 1, steps + 2, steps + 3):
            if source <= reach(which, direction) and BEFORE[source] == steps:
                arrived("z", which, direction, source)
                total += zgot[which, 0 if direction == 1 else 1, steps // 3, source - steps - 1].astype(F32)
        return total

    def zstep(which, steps):
        for side, direction in enumerate((1, -1)):
            total = part[which, chunk_rows(direction, steps), :].astype(F32)
            zsum[which, side, steps // 3 - 1] = zadd(which, direction, steps, total).astype(BF16)
            zsend(which, direction, steps, zsum.at[which, side, steps // 3 - 1])

    def zend(which):
        total = part[which, chunk_rows(1, 0), :].astype(F32)
        for direction in (1, -1):
            total = zadd(which, direction, 0, total)
        outs[which] = total.astype(BF16)
        return local(outs.at[which], (layer_out, grad_tokens)[which])

    def weight_grad(which):
        own = ins[1 - which, :, own_cols]
        for k in range(2):
            if which == 0:
                value = lax.dot_general(full[0, k], own, (((0,), (0,)), ((), ())), preferred_element_type=F32)
                gwo[pl.ds(k * HH, HH), :] = value.astype(BF16)
            else:
                value = lax.dot_general(own, full[1, k], (((0,), (0,)), ((), ())), preferred_element_type=F32)
                gwi[:, pl.ds(k * HH, HH)] = value.astype(BF16)
        return local(gwo, grad_w_out) if which == 0 else local(gwi, grad_w_in)

    for steps in FIRST:
        pass_on(0, steps)
        pass_on(1, steps)
    own_half, other_half = (pl.ds(pl.multiple_of(i * HH, 128), HH) for i in (c, other))

    own_weights = [
        local(w_in.at[:, own_half], wi_pair.at[pl.ds(pl.multiple_of(c * W, 128), W)]),
        local(w_out.at[own_half], wo_pair.at[:, own_cols]),
    ]
    last = []
    chunk_in(0, 2)
    pass_on(0, 4)
    chunk_in(1, 2)
    pass_on(1, 4)
    pass_on(0, 3)
    pass_on(1, 3)
    send(("w", 0), w_in.at[:, other_half], wi_pair.at[pl.ds(pl.multiple_of(c * W, 128), W)], pair)
    send(("w", 1), w_out.at[other_half], wo_pair.at[:, own_cols], pair)
    chunk_in(0, 1)
    chunk_in(1, 1)
    chunk_in(0, 4)
    pass_on(0, 6)
    chunk_in(1, 4)
    pass_on(1, 6)
    pass_on(0, 5)
    pass_on(1, 5)
    chunk_in(0, 3)
    to_pair(0, 0)
    chunk_in(1, 3)
    to_pair(1, 0)
    chunk_in(0, 6)
    pass_on(0, 8)
    chunk_in(1, 6)
    pass_on(1, 8)
    pass_on(0, 7)
    pass_on(1, 7)
    for copy in own_weights:
        copy.wait()
    arrived("w", 0)
    arrived("pair", 0, 0)
    product(0, 0)
    scatter1(0, 0)
    arrived("w", 1)
    full_weights = [local(w_in, wi), local(w_out, wo)]
    arrived("pair", 1, 0)
    product(1, 0)
    scatter1(1, 0)
    chunk_in(0, 5)
    chunk_in(1, 5)
    chunk_in(0, 8)
    chunk_in(1, 8)
    chunk_in(0, 7)
    to_pair(0, 1)
    chunk_in(1, 7)
    to_pair(1, 1)
    scatter2(0, 0)
    arrived("pair", 0, 1)
    product(0, 1)
    scatter1(0, 1)
    scatter2(1, 0)
    arrived("pair", 1, 1)
    product(1, 1)
    scatter1(1, 1)
    finish(0, 0)
    scatter2(0, 1)
    finish(1, 0)
    scatter2(1, 1)
    finish(0, 1)
    gather2(0, 0)
    finish(1, 1)
    gather2(0, 1)
    gather2(1, 0)
    gather2(1, 1)
    gather3(0, 0)
    for copy in full_weights:
        copy.wait()
    project(0, 0)
    zraw(0, 0)
    gather3(0, 1)
    project(0, 1)
    zraw(0, 1)
    last.append(weight_grad(0))
    gather3(1, 0)
    project(1, 0)
    zraw(1, 0)
    gather3(1, 1)
    zstep(0, 6)
    project(1, 1)
    zraw(1, 1)
    zstep(1, 6)
    zstep(0, 3)
    sent()
    zstep(1, 3)
    last.append(weight_grad(1))
    last.append(zend(0))
    last.append(zend(1))
    sent()
    for copy in last:
        copy.wait()


def to_outputs(*refs):
    sources, targets, held, sems = refs[:4], refs[4:8], refs[8:12], refs[12]
    blocks = [(i, pl.ds(k * held[i].shape[0] // 4, held[i].shape[0] // 4)) for k in range(4) for i in (2, 3)]
    blocks += [(0, pl.ds(0, CHUNK)), (1, pl.ds(0, CHUNK))]
    first = [pltpu.make_async_copy(sources[i].at[r], held[i].at[r], sems.at[0, n]) for n, (i, r) in enumerate(blocks)]
    second = [pltpu.make_async_copy(held[i].at[r], targets[i].at[r], sems.at[1, n]) for n, (i, r) in enumerate(blocks)]
    for copy in first:
        copy.start()
    for before, after in zip(first, second):
        before.wait()
        after.start()
    for copy in second:
        copy.wait()


def shards(tokens, cotangent, w_in, w_out):
    results = kernel_call(tokens, cotangent, w_in, w_out)
    return pl.pallas_call(
        to_outputs,
        out_shape=tuple(jax.ShapeDtypeStruct(r.shape, r.dtype) for r in results),
        in_specs=[pl.BlockSpec(memory_space=pl.ANY)] * 4,
        out_specs=(pl.BlockSpec(memory_space=pl.ANY),) * 4,
        scratch_shapes=[*(pltpu.VMEM(r.shape, r.dtype) for r in results), pltpu.SemaphoreType.DMA((2, 10))],
        name="to_outputs",
    )(*results)


def kernel_call(tokens, cotangent, w_in, w_out):
    copies = 2 * 15 + 2 * GROUPS + 2 + 2 * GROUPS * 26 + 2 * 15
    anywhere = pl.BlockSpec(memory_space=pl.ANY)
    shape = jax.ShapeDtypeStruct
    return pl.pallas_call(
        body,
        out_shape=(
            shape((CHUNK, W), BF16), shape((CHUNK, W), BF16), shape((W, H), BF16), shape((H, W), BF16),
        ),
        in_specs=[pl.BlockSpec(memory_space=pltpu.HBM)] * 4,
        out_specs=(anywhere,) * 4,
        scratch_shapes=[
            pltpu.VMEM((2, TOKENS, CW), BF16),
            pltpu.VMEM((W, H), BF16),
            pltpu.VMEM((H, W), BF16),
            pltpu.VMEM((CW, HH), BF16),
            pltpu.VMEM((HH, CW), BF16),
            pltpu.VMEM((2, TOKENS, HH), BF16),
            pltpu.VMEM((2, GROUPS, 2, 3, PART, W), BF16),
            pltpu.VMEM((2, GROUPS, 2, PART, W), BF16),
            pltpu.VMEM((2, GROUPS, 2, 3, PIECE, W), BF16),
            pltpu.VMEM((2, 2, TOKENS, HH), BF16),
            pltpu.VMEM((2, TOKENS, W), BF16),
            pltpu.VMEM((2, 2, 3, 3, CHUNK, W), BF16),
            pltpu.VMEM((2, 2, 2, CHUNK, W), BF16),
            pltpu.VMEM((2, CHUNK, W), BF16),
            pltpu.VMEM((W, H), BF16),
            pltpu.VMEM((H, W), BF16),
            pltpu.SemaphoreType.DMA((10,)),
            pltpu.SemaphoreType.DMA((copies,)),
            pltpu.SemaphoreType.DMA((copies,)),
        ],
        compiler_params=pltpu.CompilerParams(
            collective_id=0, has_side_effects=True, vmem_limit_bytes=60 * 2**20
        ),
        cost_estimate=pl.CostEstimate(flops=12 * TOKENS * W * H, bytes_accessed=10 * W * H, transcendentals=0),
        name="ffn",
    )(tokens, cotangent, w_in, w_out)


def solution(mesh):
    return jax.shard_map(
        shards,
        mesh=mesh,
        in_specs=(P("col", "row"), P("col", "row"), P("row", "col"), P("col", "row")),
        out_specs=(P("col", "row"), P("col", "row"), P("row", "col"), P("col", "row")),
        check_vma=False,
    )
```
